128 devices in a mesh: rows: 8 (over z, core), cols: 16 (over y, x).
Axes of the slice: x: 4, y: 4, z: 4, core: 2. Of those that a mesh axis runs over, the one named last changes fastest.
Arguments:
- vectors: bfloat16 [16, 524288], P(None, ('rows', 'cols')), may hold values from -6 to 6
- tree_order: int32 [524288], P(('rows', 'cols')), may hold values from 0 to 524287, as said below
- near_blocks: bfloat16 [2048, 8, 256, 256], P(('rows', 'cols')), may hold values from -0.125 to 0.125
- near_index: int32 [2048, 8], P(('rows', 'cols')), may hold values from 0 to 2047, as said below
- leaf_basis: bfloat16 [2048, 64, 256], P(('rows', 'cols')), may hold values from -0.375 to 0.375
- leaf_coupling: bfloat16 [2048, 16, 64, 64], P(('rows', 'cols')), may hold values from -0.1875 to 0.1875
- leaf_far: int32 [2048, 16], P(('rows', 'cols')), may hold values from 0 to 2047, as said below
- leaf_transfer: bfloat16 [2048, 64, 64], P(('rows', 'cols')), may hold values from -0.375 to 0.375
- node_coupling: bfloat16 [128, 8, 64, 64], P(('rows', 'cols')), may hold values from -0.25 to 0.25
- node_far: int32 [128, 8], P(('rows', 'cols')), may hold values from 0 to 127, as said below
- node_transfer: bfloat16 [128, 64, 64], P(('rows', 'cols')), may hold values from -0.375 to 0.375
- slab_coupling: bfloat16 [8, 2, 64, 64], P('rows'), may hold values from -0.5 to 0.5
- slab_far_partners: int32 [8, 2], P('rows'), may hold values from 0 to 7, as said below
Outputs:
- product: bfloat16 [16, 524288], P(None, ('rows', 'cols'))
The draws below stay inside these ranges and needn't reach their ends.
Inputs may be any that keep to these rules, and one draw needn't show every extreme that they name: `tree_order`: a permutation that maps each aligned block of 4096 positions onto the same block of initial indices. `near_index`: the partners of a leaf are distinct leaves of its own aligned block of 256 leaves; the first is the leaf itself. `leaf_far`: distinct leaves of the leaf's own aligned block of 256 leaves, none of them among its near partners. `node_far`: distinct device-level clusters other than the cluster itself. `slab_far_partners`: distinct slab-level clusters other than the cluster itself.
All inputs are finite; a program needn't handle non-finite values.
Results may differ from the reference program's by a relative error of at most 0.00125.
Values may be sent and summed in bfloat16 or wider, within the bound.
A program may use at most 128 MiB of HBM per device.

```python
import jax
import jax.numpy as jnp
from jax import lax

LEAF_PTS = 256
RANK = 64
RHS = 16
LEAF_DEV = 16
NEAR = 8
LEAF_FAR = 16
NODE_FAR = 8
SLAB_FAR = 2
PTS_DEV = 4096
SLAB_LEAVES = 256
LEAVES = 2048
POINTS = 524288
N_ROWS = 8
N_COLS = 16
DEVICES = 128


def slab_lists(key):
    columns = jnp.arange(SLAB_LEAVES, dtype=jnp.int32)
    scores = jax.random.randint(key, (LEAVES, SLAB_LEAVES), 0, 1 << 16) * SLAB_LEAVES + columns[None, :]
    own_slot = jnp.arange(LEAVES, dtype=jnp.int32) % SLAB_LEAVES
    scores = jnp.where(columns[None, :] == own_slot[:, None], 1 << 30, scores)
    discarded_value, chosen = lax.top_k(scores, NEAR + LEAF_FAR)
    slab_start = jnp.arange(LEAVES, dtype=jnp.int32) // SLAB_LEAVES * SLAB_LEAVES
    return (chosen + slab_start[:, None]).astype(jnp.int32)


def other_lists(key, cluster_count, pick_count):
    columns = jnp.arange(cluster_count, dtype=jnp.int32)
    scores = jax.random.randint(key, (cluster_count, cluster_count), 0, 1 << 16) * cluster_count + columns[None, :]
    scores = jnp.where(columns[None, :] == columns[:, None], -1, scores)
    discarded_value, chosen = lax.top_k(scores, pick_count)
    return chosen.astype(jnp.int32)


def draw_tree_order(key, part):
    key = jax.random.fold_in(key, 3)
    owners = POINTS // PTS_DEV
    scores = jax.random.randint(key, (owners, PTS_DEV), 0, 1 << 16) * PTS_DEV + jnp.arange(PTS_DEV, dtype=jnp.int32)[None, :]
    ranked = jnp.argsort(scores, axis=1, stable=True).astype(jnp.int32)
    ranked = ranked + jnp.arange(owners, dtype=jnp.int32)[:, None] * PTS_DEV
    return ranked.reshape(POINTS).astype(jnp.int32)


def draw_near_index(key, part):
    lists = slab_lists(key)
    return lists[:, :NEAR]


def draw_leaf_far(key, part):
    lists = slab_lists(key)
    return lists[:, NEAR:]


def draw_node_far(key, part):
    key = jax.random.fold_in(key, 5)
    return other_lists(key, LEAVES // LEAF_DEV, NODE_FAR)


def draw_slab_far_partners(key, part):
    key = jax.random.fold_in(key, 7)
    return other_lists(key, LEAVES // SLAB_LEAVES, SLAB_FAR)


def block_levels(key, dims, split, least, largest):
    level = 1.0
    for axis_at, blocks in split:
        steps = jax.random.uniform(jax.random.fold_in(jax.random.fold_in(key, 6), axis_at), (blocks,), jnp.float32, least / len(split), largest / len(split))
        level = level * jnp.repeat(jnp.exp(steps), dims[axis_at] // blocks).reshape((-1,) + (1,) * (len(dims) - 1 - axis_at))
    return level


def normal_values(own_key, dims, spread, most, cuts=(), held_as=jnp.bfloat16):
    array = spread * jax.random.normal(own_key, dims, jnp.float32)
    if cuts:
        array = array * block_levels(own_key, dims, cuts, -0.22, 0.18)
    return jnp.clip(array, -most, most).astype(held_as)


def setup_inputs(seed: int = 0) -> dict:
    keys = jax.random.split(jax.random.key(seed), 14)
    return {
        "vectors": normal_values(keys[0], (RHS, POINTS), 1.0, 6.0, ((1, 128),)),
        "tree_order": draw_tree_order(jax.random.fold_in(keys[13], 71), 0),
        "near_blocks": normal_values(keys[2], (LEAVES, NEAR, LEAF_PTS, LEAF_PTS), (LEAF_PTS * NEAR) ** -0.5, 0.125, ((0, 128),)),
        "near_index": draw_near_index(jax.random.fold_in(keys[13], 71), 0),
        "leaf_basis": normal_values(keys[4], (LEAVES, RANK, LEAF_PTS), LEAF_PTS ** -0.5, 0.375, ((0, 128),)),
        "leaf_coupling": normal_values(keys[5], (LEAVES, LEAF_FAR, RANK, RANK), (RANK * LEAF_FAR) ** -0.5, 0.1875, ((0, 128),)),
        "leaf_far": draw_leaf_far(jax.random.fold_in(keys[13], 71), 0),
        "leaf_transfer": normal_values(keys[7], (LEAVES, RANK, RANK), (RANK * LEAF_DEV // 4 + RANK // 4) ** -0.5, 0.375, ((0, 128),)),
        "node_coupling": normal_values(keys[8], (DEVICES, NODE_FAR, RANK, RANK), (RANK * NODE_FAR) ** -0.5, 0.25, ((0, 128),)),
        "node_far": draw_node_far(jax.random.fold_in(keys[13], 71), 0),
        "node_transfer": normal_values(keys[10], (DEVICES, RANK, RANK), (RANK * N_COLS // 4) ** -0.5, 0.375, ((0, 128),)),
        "slab_coupling": normal_values(keys[11], (N_ROWS, SLAB_FAR, RANK, RANK), (RANK * SLAB_FAR) ** -0.5, 0.5, ((0, 8),)),
        "slab_far_partners": draw_slab_far_partners(jax.random.fold_in(keys[13], 71), 0),
    }


def reference(vectors, tree_order, near_blocks, near_index, leaf_basis, leaf_coupling, leaf_far, leaf_transfer, node_coupling, node_far, node_transfer, slab_coupling, slab_far_partners):
    highest = lax.Precision.HIGHEST
    node_count = LEAVES // LEAF_DEV
    slab_count = LEAVES // SLAB_LEAVES
    tree_vectors = vectors[:, tree_order]
    leaf_vectors = tree_vectors.reshape(RHS, LEAVES, LEAF_PTS)

    def near_row(operands):
        block_list, partners = operands
        selected_entries = leaf_vectors[:, partners, :].astype(jnp.float32)
        return jnp.einsum('hmc,mdc->hd', selected_entries, block_list.astype(jnp.float32))

    near_part = lax.map(near_row, (near_blocks, near_index))
    leaf_coef = jnp.einsum('rlb,lkb->lrk', leaf_vectors.astype(jnp.float32), leaf_basis.astype(jnp.float32))
    leaf_out = jnp.einsum('lsrm,lskm->lrk', leaf_coef[leaf_far], leaf_coupling.astype(jnp.float32), precision=highest)
    up_leaf = leaf_transfer.astype(jnp.float32).reshape(node_count, LEAF_DEV, RANK, RANK)
    node_coef = jnp.einsum('dcrm,dckm->drk', leaf_coef.reshape(node_count, LEAF_DEV, RHS, RANK), up_leaf, precision=highest)
    node_out = jnp.einsum('dsrm,dskm->drk', node_coef[node_far], node_coupling.astype(jnp.float32), precision=highest)
    upward_node_coef = node_transfer.astype(jnp.float32).reshape(slab_count, N_COLS, RANK, RANK)
    slab_coef = jnp.einsum('gcrm,gckm->grk', node_coef.reshape(slab_count, N_COLS, RHS, RANK), upward_node_coef, precision=highest)
    slab_out = jnp.einsum('gsrm,gskm->grk', slab_coef[slab_far_partners], slab_coupling.astype(jnp.float32), precision=highest)
    node_out = node_out + jnp.einsum('grk,gckm->gcrm', slab_out, upward_node_coef, precision=highest).reshape(node_count, RHS, RANK)
    leaf_out = leaf_out + jnp.einsum('drk,dckm->dcrm', node_out, up_leaf, precision=highest).reshape(LEAVES, RHS, RANK)
    far_part = jnp.einsum('lrk,lkb->lrb', leaf_out, leaf_basis.astype(jnp.float32), precision=highest)
    tree_product = (near_part + far_part).transpose(1, 0, 2).reshape(RHS, POINTS)
    product = jnp.zeros((RHS, POINTS), jnp.float32).at[:, tree_order].set(tree_product)
    return product.astype(jnp.bfloat16)
```

```python
import jax
import jax.numpy as jnp
from jax import lax
from jax.experimental import pallas as pl
from jax.experimental.pallas import tpu as pltpu
from jax.sharding import PartitionSpec as P

MESH = pl.DeviceIdType.MESH
F32 = jnp.float32
BF16 = jnp.bfloat16

NT = (((1,), (1,)), ((), ()))
NN = (((1,), (0,)), ((), ()))


def dot(a, b, dims):
    return lax.dot_general(a, b, dims, preferred_element_type=F32)


def split2(v):
    high = v.astype(BF16)
    low = (v - high.astype(F32)).astype(BF16)
    return high, low


def dot2(v, b, dims):
    high, low = split2(v)
    rows = v.shape[0]
    both = dot(jnp.concatenate([high, low], axis=0), b, dims)
    return both[:rows] + both[rows:]


def shifted(col, dim, by):
    x, y = col % 4, col // 4
    if dim == 0:
        return y * 4 + (x + by) % 4
    return ((y + by) % 4) * 4 + x


def kernel(
    vec_hbm, ord_hbm, near_hbm, basis_hbm, coup_hbm, ltran_hbm, ncoup_hbm, ntran_hbm, scoup_hbm,
    near_idx, far_idx, node_idx, slab_idx,
    out_ref,
    vec, order, near, basis, coup, ltran, ncoup, ntran, scoup,
    onehot, wdup, x_low, x_high, coef_buf, node_buf, row_buf, near_acc, node_out_ref,
    in_sem, near_sem, send_sem, recv_sem, nsend, nrecv,
):
    col = lax.axis_index("cols")
    row = lax.axis_index("rows")
    my_x, my_y = col % 4, col // 4

    def fetch(src, dst, k):
        copy = pltpu.make_async_copy(src, dst, in_sem.at[k])
        copy.start()
        return copy

    c_vec = fetch(vec_hbm, vec, 0)
    c_ord = fetch(ord_hbm, order, 1)
    c_basis = fetch(basis_hbm, basis, 2)
    c_ltran = fetch(ltran_hbm, ltran, 3)
    c_ntran = fetch(ntran_hbm, ntran, 4)

    barrier = pltpu.get_barrier_semaphore()
    partners = [{"cols": shifted(col, dim, by)} for dim in (0, 1) for by in (1, 2, 3)]
    zrow = [(row + 2 * by) % 8 for by in (1, 2, 3)]
    other_core = row + 1 - 2 * (row % 2)
    partners += [{"rows": r} for r in zrow] + [{"rows": other_core}]
    for p in partners:
        pl.semaphore_signal(barrier, inc=1, device_id=p, device_id_type=MESH)

    c_ncoup = fetch(ncoup_hbm, ncoup, 5)
    c_scoup = fetch(scoup_hbm, scoup, 6)
    c_coup = fetch(coup_hbm, coup, 7)
    c_near = []
    for q in range(4):
        copy = pltpu.make_async_copy(
            near_hbm.at[pl.ds(4 * q, 4)], near.at[pl.ds(4 * q, 4)], near_sem.at[q]
        )
        copy.start()
        c_near.append(copy)

    c_vec.wait()
    c_ord.wait()
    lhs = jnp.concatenate([vec[:, h * 256:(h + 1) * 256] for h in range(16)], axis=0)
    level = lax.broadcasted_iota(jnp.int32, (256, 256), 0)

    def permute(leaf):
        local = order[:, leaf * 256:(leaf + 1) * 256] % 4096
        low = jnp.broadcast_to(local % 256, (256, 256))
        hot = jnp.where(low == level, 1.0, 0.0).astype(BF16)
        onehot[leaf] = hot
        part = dot(lhs, hot, NN)
        high = local // 256
        x = jnp.zeros((16, 256), F32)
        for h in range(16):
            x = x + jnp.where(high == h, part[h * 16:(h + 1) * 16], 0.0)
        return x.astype(BF16)

    own = col * 16
    slab_buf = (x_low, x_high, coef_buf)
    leaf_x = []
    for leaf in range(16):
        x = permute(leaf)
        x_low[own + leaf] = x[:, :128]
        x_high[own + leaf] = x[:, 128:]

    pl.semaphore_wait(barrier, len(partners))

    sent = []

    def chunk_copy(stage, chunk, first, count, to, k):
        span = slab_buf[stage].at[pl.ds(chunk * 16 + first, count)]
        return pltpu.make_async_remote_copy(
            span, span, send_sem.at[stage * 40 + k], recv_sem.at[stage * 40 + k],
            device_id={"cols": to}, device_id_type=MESH,
        )

    def send(stage, chunk, first, count, to, k):
        copy = chunk_copy(stage, chunk, first, count, to, k)
        copy.start()
        sent.append(copy)

    def arrived(stage, chunk, first, count, k):
        chunk_copy(stage, chunk, first, count, shifted(col, 0, 1), k).wait_recv()

    def at(half, a, b):
        return shifted(shifted(col, half, a), 1 - half, b)

    def key(half, phase, a, t):
        return half * 20 + (0 if phase == 0 else 4 + 4 * a) + t

    def dim_of(half, phase):
        return half if phase == 0 else 1 - half

    def put(stage, half, phase, a):
        d = dim_of(half, phase)
        chunk = at(half, a, 0) if phase else col
        send(stage, chunk, half * 8, 8, shifted(col, d, 1), key(half, phase, a, 0))
        send(stage, chunk, half * 8, 8, shifted(col, d, 3), key(half, phase, a, 1))

    def source(half, phase, a, by):
        return at(half, a, by) if phase else at(half, by, 0)

    def forward(stage, half, phase, a):
        d = dim_of(half, phase)
        chunk = source(half, phase, a, 3)
        arrived(stage, chunk, half * 8, 8, key(half, phase, a, 0))
        send(stage, chunk, half * 8, 4, shifted(col, d, 1), key(half, phase, a, 2))
        chunk = source(half, phase, a, 1)
        arrived(stage, chunk, half * 8, 8, key(half, phase, a, 1))
        send(stage, chunk, half * 8 + 4, 4, shifted(col, d, 3), key(half, phase, a, 3))

    def finish(stage, half, phase, a):
        chunk = source(half, phase, a, 2)
        arrived(stage, chunk, half * 8, 4, key(half, phase, a, 2))
        arrived(stage, chunk, half * 8 + 4, 4, key(half, phase, a, 3))

    def step0(stage):
        for half in (0, 1):
            put(stage, half, 0, 0)
        for half in (0, 1):
            put(stage, half, 1, 0)

    def step1(stage):
        for half in (0, 1):
            forward(stage, half, 0, 0)
        for a in (1, 3):
            for half in (0, 1):
                put(stage, half, 1, a)

    def step2(stage):
        for half in (0, 1):
            finish(stage, half, 0, 0)
        for half in (0, 1):
            put(stage, half, 1, 2)
        for half in (0, 1):
            forward(stage, half, 1, 0)

    def step3(stage, a):
        for half in (0, 1):
            forward(stage, half, 1, a)

    def step4(stage):
        for a in (0, 1, 3, 2):
            for half in (0, 1):
                finish(stage, half, 1, a)

    step0(0)

    c_basis.wait()
    c_ltran.wait()
    c_ntran.wait()
    node_coef = jnp.zeros((16, 64), F32)
    for leaf in range(16):
        coef = dot(x_low[own + leaf], basis[leaf, :, :128], NT) + dot(
            x_high[own + leaf], basis[leaf, :, 128:], NT
        )
        high, low = split2(coef)
        coef_buf[own + leaf] = jnp.concatenate([high, low], axis=1)
        node_coef = node_coef + dot2(coef, ltran[leaf], NT)
    node_term = dot2(node_coef, ntran[0], NT)

    def node_copy(src, k, to):
        return pltpu.make_async_remote_copy(
            src, src, nsend.at[k], nrecv.at[k], device_id=to, device_id_type=MESH
        )

    def node_send(src, k, to):
        copy = node_copy(src, k, to)
        copy.start()
        sent.append(copy)

    node_buf[my_y, my_x] = jnp.concatenate([node_coef, node_term], axis=1)
    for by in (1, 3, 2):
        node_send(node_buf.at[my_y, my_x], by - 1, {"cols": shifted(col, 0, by)})
    step0(1)
    step1(0)
    for by in (1, 3, 2):
        node_copy(node_buf.at[my_y, (my_x + 4 - by) % 4], by - 1, partners[0]).wait_recv()
    for by in (1, 3, 2):
        node_send(node_buf.at[my_y], 2 + by, {"cols": shifted(col, 1, by)})
    step2(0)
    for a in (1, 3, 2):
        step3(0, a)
    for by in (1, 3, 2):
        node_copy(node_buf.at[(my_y + 4 - by) % 4], 2 + by, partners[0]).wait_recv()
    slab_coef = jnp.zeros((16, 64), F32)
    for m in range(8):
        left, right = node_buf[m // 2, m % 2 * 2], node_buf[m // 2, m % 2 * 2 + 1]
        row_buf[row, m] = jnp.concatenate([left[:, :64], right[:, :64]], axis=1)
        slab_coef = slab_coef + (left[:, 64:] + right[:, 64:])
    row_buf[row, 8] = jnp.concatenate([slab_coef, slab_coef], axis=1)
    for n, by in enumerate((1, 3, 2)):
        node_send(row_buf.at[row], 6 + n, {"rows": (row + 2 * by) % 8})
    node_send(row_buf.at[row], 9, {"rows": other_core})
    step1(1)
    step4(0)
    step0(2)

    def near_part(stage, first, count):
        def body(leaf, carry):
            acc = near_acc[leaf] if stage else jnp.zeros((16, 256), F32)
            for s in range(8):
                x = slab_buf[stage][near_idx[s, leaf] % 256]
                acc = acc + dot(x, near[leaf, s, :, stage * 128:stage * 128 + 128], NT)
            near_acc[leaf] = acc
            return carry

        lax.fori_loop(first, first + count, body, 0)

    for copy in c_near:
        copy.wait()
    near_part(0, 0, 4)
    step2(1)
    step1(2)
    near_part(0, 4, 4)
    step3(1, 1)
    step3(1, 3)
    near_part(0, 8, 4)
    step3(1, 2)
    near_part(0, 12, 4)

    for n, by in enumerate((1, 3, 2)):
        node_copy(row_buf.at[(row + 8 - 2 * by) % 8], 6 + n, partners[0]).wait_recv()
        node_send(row_buf.at[(row + 8 - 2 * by) % 8], 10 + n, {"rows": other_core})
    step4(1)
    step2(2)

    c_coup.wait()

    def dup_body(leaf, carry):
        for s in range(16):
            m = coup[leaf, s]
            wdup[leaf, :, s * 128:(s + 1) * 128] = jnp.concatenate([m, m], axis=1)
        return carry

    lax.fori_loop(0, 16, dup_body, 0)

    near_part(1, 0, 4)
    step3(2, 1)
    step3(2, 3)
    near_part(1, 4, 4)
    step3(2, 2)
    near_part(1, 8, 8)

    node_copy(row_buf.at[other_core], 9, partners[0]).wait_recv()
    for n, by in enumerate((1, 3, 2)):
        node_copy(row_buf.at[(other_core + 8 - 2 * by) % 8], 10 + n, partners[0]).wait_recv()
    c_ncoup.wait()
    c_scoup.wait()
    slab_out = jnp.zeros((16, 64), F32)
    for s in range(2):
        slab_out = slab_out + dot2(row_buf[slab_idx[0, s], 8][:, :64], scoup[0, s], NT)
    node_out = dot2(slab_out, ntran[0], NN)
    lane = lax.broadcasted_iota(jnp.int32, (16, 128), 1)
    for s in range(8):
        d = node_idx[0, s]
        both = row_buf[d // 16, d % 16 // 2]
        both = jnp.where(lane // 64 == d % 2, both, 0.0)
        pair = jnp.concatenate([ncoup[0, s], ncoup[0, s]], axis=1)
        node_out = node_out + dot2(both, pair, NT)
    node_out_ref[...] = node_out

    step4(2)

    level_row = lax.broadcasted_iota(jnp.int32, (1, 256), 1)

    def last_body(leaf, acc):
        lhs = jnp.concatenate([coef_buf[far_idx[leaf, s] % 256] for s in range(16)], axis=1)
        leaf_out = dot(lhs, wdup[leaf], NT)
        leaf_out = leaf_out + dot2(node_out_ref[...], ltran[leaf], NN)
        tree = near_acc[leaf] + dot2(leaf_out, basis[leaf], NN)
        local = order[:, pl.ds(pl.multiple_of(leaf * 256, 256), 256)] % 4096
        high = local // 256
        spread = jnp.concatenate(
            [jnp.where(high == h, tree, 0.0).astype(BF16) for h in range(16)], axis=0
        )
        return acc + dot(spread, onehot[leaf], NT)

    acc = lax.fori_loop(0, 16, last_body, jnp.zeros((256, 256), F32))
    for h in range(16):
        out_ref[:, h * 256:(h + 1) * 256] = acc[h * 16:(h + 1) * 16].astype(BF16)
    for copy in sent:
        copy.wait_send()


def on_device(
    vectors, tree_order, near_blocks, near_index, leaf_basis, leaf_coupling, leaf_far,
    leaf_transfer, node_coupling, node_far, node_transfer, slab_coupling, slab_far_partners,
):
    hbm = pl.BlockSpec(memory_space=pltpu.HBM)
    smem = pl.BlockSpec(memory_space=pltpu.SMEM)
    return pl.pallas_call(
        kernel,
        out_shape=jax.ShapeDtypeStruct((16, 4096), BF16),
        in_specs=[hbm] * 9 + [smem] * 4,
        out_specs=pl.BlockSpec(memory_space=pltpu.VMEM),
        scratch_shapes=[
            pltpu.VMEM((16, 4096), BF16),
            pltpu.VMEM((1, 4096), jnp.int32),
            pltpu.VMEM((16, 8, 256, 256), BF16),
            pltpu.VMEM((16, 64, 256), BF16),
            pltpu.VMEM((16, 16, 64, 64), BF16),
            pltpu.VMEM((16, 64, 64), BF16),
            pltpu.VMEM((1, 8, 64, 64), BF16),
            pltpu.VMEM((1, 64, 64), BF16),
            pltpu.VMEM((1, 2, 64, 64), BF16),
            pltpu.VMEM((16, 256, 256), BF16),
            pltpu.VMEM((16, 64, 2048), BF16),
            pltpu.VMEM((256, 16, 128), BF16),
            pltpu.VMEM((256, 16, 128), BF16),
            pltpu.VMEM((256, 16, 128), BF16),
            pltpu.VMEM((4, 4, 16, 128), F32),
            pltpu.VMEM((8, 9, 16, 128), F32),
            pltpu.VMEM((16, 16, 256), F32),
            pltpu.VMEM((16, 64), F32),
            pltpu.SemaphoreType.DMA((8,)),
            pltpu.SemaphoreType.DMA((4,)),
            pltpu.SemaphoreType.DMA((120,)),
            pltpu.SemaphoreType.DMA((120,)),
            pltpu.SemaphoreType.DMA((13,)),
            pltpu.SemaphoreType.DMA((13,)),
        ],
        compiler_params=pltpu.CompilerParams(
            collective_id=0, has_side_effects=True, vmem_limit_bytes=56 << 20
        ),
    )(
        vectors, tree_order.reshape(1, 4096), near_blocks, leaf_basis, leaf_coupling, leaf_transfer,
        node_coupling, node_transfer, slab_coupling,
        near_index.T, leaf_far, node_far, slab_far_partners,
    )


def solution(mesh):
    whole = ("rows", "cols")
    return jax.shard_map(
        on_device,
        mesh=mesh,
        in_specs=(
            P(None, whole), P(whole), P(whole), P(whole), P(whole), P(whole), P(whole),
            P(whole), P(whole), P(whole), P(whole), P("rows"), P("rows"),
        ),
        out_specs=P(None, whole),
        check_vma=False,
    )
```

```python
import jax
import jax.numpy as jnp
from jax import lax
from jax.experimental import pallas as pl
from jax.experimental.pallas import tpu as pltpu
from jax.sharding import PartitionSpec as P

MESH = pl.DeviceIdType.MESH
F32 = jnp.float32
BF16 = jnp.bfloat16

NT = (((1,), (1,)), ((), ()))
NN = (((1,), (0,)), ((), ()))

PLAN = (
    "n0", "x8", "x9", "n1", "c8", "c9", "t0", "x1", "n2", "c1", "t1", "x2", "c2", "t2", "x3",
    "c3", "t3", "x4", "c4", "t4", "x5", "c5", "t5", "x6", "c6", "t6", "t7", "n3", "d0", "d1",
    "d2", "d3", "o", "x7", "N0", "N1", "N2", "N3", "c7", "F", "n4", "L",
)


def dot(a, b, dims):
    return lax.dot_general(a, b, dims, preferred_element_type=F32)


def split2(v):
    high = v.astype(BF16)
    low = (v - high.astype(F32)).astype(BF16)
    return high, low


def dot2(v, b, dims):
    high, low = split2(v)
    rows = v.shape[0]
    both = dot(jnp.concatenate([high, low], axis=0), b, dims)
    return both[:rows] + both[rows:]


def shifted(col, dim, by):
    x, y = col % 4, col // 4
    if dim == 0:
        return y * 4 + (x + by) % 4
    return ((y + by) % 4) * 4 + x


def kernel(
    vec_hbm, ord_hbm, near_hbm, basis_hbm, coup_hbm, ltran_hbm, ncoup_hbm, ntran_hbm, scoup_hbm,
    near_idx, far_idx, node_idx, slab_idx,
    out_ref,
    vec, order, near, basis, coup, ltran, ncoup, ntran, scoup,
    onehot, coup_t, x_buf, coef_buf, node_buf, row_buf, near_acc, leaf_acc, spread,
    in_sem, near_sem, send_sem, recv_sem, nsend, nrecv,
):
    col = lax.axis_index("cols")
    row = lax.axis_index("rows")
    my_x, my_y = col % 4, col // 4

    barrier = pltpu.get_barrier_semaphore()
    partners = [{"cols": shifted(col, dim, by)} for dim in (0, 1) for by in (1, 2, 3)]
    other_core = row + 1 - 2 * (row % 2)
    partners += [{"rows": (row + 2 * by) % 8} for by in (1, 2, 3)] + [{"rows": other_core}]
    for p in partners:
        pl.semaphore_signal(barrier, inc=1, device_id=p, device_id_type=MESH)

    def fetch(src, dst, sem):
        copy = pltpu.make_async_copy(src, dst, sem)
        copy.start()
        return copy

    c_vec = fetch(vec_hbm, vec, in_sem.at[0])
    c_ord = fetch(ord_hbm, order, in_sem.at[1])
    c_basis = fetch(basis_hbm, basis, in_sem.at[2])
    c_ltran = fetch(ltran_hbm, ltran, in_sem.at[3])
    c_ntran = fetch(ntran_hbm, ntran, in_sem.at[4])
    c_near = [
        fetch(near_hbm.at[pl.ds(2 * q, 2)], near.at[pl.ds(2 * q, 2)], near_sem.at[q])
        for q in range(8)
    ]
    c_coup = fetch(coup_hbm, coup, in_sem.at[7])
    c_ncoup = fetch(ncoup_hbm, ncoup, in_sem.at[5])
    c_scoup = fetch(scoup_hbm, scoup, in_sem.at[6])

    sent = []
    buffers = (x_buf, coef_buf)

    def chunk_copy(stage, chunk, first, count, to, k):
        span = buffers[stage].at[pl.ds(chunk * 16 + first, count)]
        return pltpu.make_async_remote_copy(
            span, span, send_sem.at[stage * 40 + k], recv_sem.at[stage * 40 + k],
            device_id={"cols": to}, device_id_type=MESH,
        )

    def send(stage, chunk, first, count, to, k):
        copy = chunk_copy(stage, chunk, first, count, to, k)
        copy.start()
        sent.append(copy)

    def arrived(stage, chunk, first, count, k):
        chunk_copy(stage, chunk, first, count, shifted(col, 0, 1), k).wait_recv()

    def at(half, a, b):
        return shifted(shifted(col, half, a), 1 - half, b)

    def key(half, phase, a, t):
        return half * 20 + (0 if phase == 0 else 4 + 4 * a) + t

    def dim_of(half, phase):
        return half if phase == 0 else 1 - half

    def put(stage, half, phase, a):
        d = dim_of(half, phase)
        chunk = at(half, a, 0) if phase else col
        send(stage, chunk, half * 8, 8, shifted(col, d, 1), key(half, phase, a, 0))
        send(stage, chunk, half * 8, 8, shifted(col, d, 3), key(half, phase, a, 1))

    def source(half, phase, a, by):
        return at(half, a, by) if phase else at(half, by, 0)

    def forward(stage, half, phase, a):
        d = dim_of(half, phase)
        chunk = source(half, phase, a, 3)
        arrived(stage, chunk, half * 8, 8, key(half, phase, a, 0))
        send(stage, chunk, half * 8, 4, shifted(col, d, 1), key(half, phase, a, 2))
        chunk = source(half, phase, a, 1)
        arrived(stage, chunk, half * 8, 8, key(half, phase, a, 1))
        send(stage, chunk, half * 8 + 4, 4, shifted(col, d, 3), key(half, phase, a, 3))

    def finish(stage, half, phase, a):
        chunk = source(half, phase, a, 2)
        arrived(stage, chunk, half * 8, 4, key(half, phase, a, 2))
        arrived(stage, chunk, half * 8 + 4, 4, key(half, phase, a, 3))

    def step(stage, number):
        for half in (0, 1):
            if number == 1:
                forward(stage, half, 0, 0)
            if number == 2:
                finish(stage, half, 0, 0)
            if number in (3, 4, 5, 6):
                forward(stage, half, 1, (0, 1, 3, 2)[number - 3])
        for half in (0, 1):
            if number in (0, 8):
                put(stage, half, 0, 0)
            if number == 1:
                put(stage, half, 1, 1)
            if number == 2:
                put(stage, half, 1, 2)
        for half in (0, 1):
            if number in (0, 9):
                put(stage, half, 1, 0)
            if number == 1:
                put(stage, half, 1, 3)
        if number == 7:
            for a in (0, 1, 3, 2):
                for half in (0, 1):
                    finish(stage, half, 1, a)

    c_vec.wait()
    c_ord.wait()
    lhs = jnp.concatenate([vec[:, h * 256:(h + 1) * 256] for h in range(16)], axis=0)
    level = lax.broadcasted_iota(jnp.int32, (256, 256), 0)
    own = col * 16

    def permute(leaf):
        local = order[:, leaf * 256:(leaf + 1) * 256] % 4096
        low = jnp.broadcast_to(local % 256, (256, 256))
        hot = jnp.where(low == level, 1.0, 0.0).astype(BF16)
        onehot[pl.ds(leaf * 256, 256)] = hot
        part = dot(lhs, hot, NN)
        high = local // 256
        x = jnp.zeros((16, 256), F32)
        for h in range(16):
            x = x + jnp.where(high == h, part[h * 16:(h + 1) * 16], 0.0)
        x_buf[own + leaf] = x.astype(BF16)

    for leaf in range(16):
        permute(leaf)

    c_basis.wait()
    c_ltran.wait()
    c_ntran.wait()
    coefs = []
    for leaf in range(16):
        coef = dot(x_buf[own + leaf], basis[leaf], NT)
        high, low = split2(coef)
        coef_buf[own + leaf] = jnp.concatenate([high, low], axis=1)
        coefs.append(coef)
    node_coef = jnp.zeros((16, 64), F32)
    for leaf in range(16):
        node_coef = node_coef + dot2(coefs[leaf], ltran[leaf], NT)
    node_term = dot2(node_coef, ntran[0], NT)
    pl.semaphore_wait(barrier, len(partners))

    def node_copy(src, k, to):
        return pltpu.make_async_remote_copy(
            src, src, nsend.at[k], nrecv.at[k], device_id=to, device_id_type=MESH
        )

    def node_send(src, k, to):
        copy = node_copy(src, k, to)
        copy.start()
        sent.append(copy)

    def node0():
        node_buf[my_y, my_x] = jnp.concatenate([node_coef, node_term], axis=1)
        for by in (1, 3, 2):
            node_send(node_buf.at[my_y, my_x], by - 1, {"cols": shifted(col, 0, by)})

    def node1():
        for by in (1, 3, 2):
            node_copy(node_buf.at[my_y, (my_x + 4 - by) % 4], by - 1, partners[0]).wait_recv()
        for by in (1, 3, 2):
            node_send(node_buf.at[my_y], 2 + by, {"cols": shifted(col, 1, by)})

    def node2():
        for by in (1, 3, 2):
            node_copy(node_buf.at[(my_y + 4 - by) % 4], 2 + by, partners[0]).wait_recv()
        slab_coef = jnp.zeros((16, 64), F32)
        for m in range(8):
            left, right = node_buf[m // 2, m % 2 * 2], node_buf[m // 2, m % 2 * 2 + 1]
            row_buf[row, m] = jnp.concatenate([left[:, :64], right[:, :64]], axis=1)
            slab_coef = slab_coef + (left[:, 64:] + right[:, 64:])
        row_buf[row, 8] = jnp.concatenate([slab_coef, slab_coef], axis=1)
        for n, by in enumerate((1, 3, 2)):
            node_send(row_buf.at[row], 6 + n, {"rows": (row + 2 * by) % 8})
        node_send(row_buf.at[row], 9, {"rows": other_core})

    def node3():
        for n, by in enumerate((1, 3, 2)):
            source_row = (row + 8 - 2 * by) % 8
            node_copy(row_buf.at[source_row], 6 + n, partners[0]).wait_recv()
            node_send(row_buf.at[source_row], 10 + n, {"rows": other_core})

    def node4():
        node_copy(row_buf.at[other_core], 9, partners[0]).wait_recv()
        for n, by in enumerate((1, 3, 2)):
            source_row = (other_core + 8 - 2 * by) % 8
            node_copy(row_buf.at[source_row], 10 + n, partners[0]).wait_recv()
        c_ncoup.wait()
        c_scoup.wait()
        slab_out = jnp.zeros((16, 64), F32)
        for s in range(2):
            slab_out = slab_out + dot2(row_buf[slab_idx[0, s], 8][:, :64], scoup[0, s], NT)
        node_out = dot2(slab_out, ntran[0], NN)
        lane = lax.broadcasted_iota(jnp.int32, (16, 128), 1)
        for s in range(8):
            d = node_idx[0, s]
            both = row_buf[d // 16, d % 16 // 2]
            both = jnp.where(lane // 64 == d % 2, both, 0.0)
            pair = jnp.concatenate([ncoup[0, s], ncoup[0, s]], axis=1)
            node_out = node_out + dot2(both, pair, NT)
        for leaf in range(16):
            leaf_acc[leaf] = leaf_acc[leaf] + dot2(node_out, ltran[leaf], NN)

    def loop(first, count, body):
        def wrapped(k, carry):
            body(k)
            return carry

        lax.fori_loop(first, first + count, wrapped, 0)

    def turn_near(q):
        c_near[q].wait()

        def body(leaf):
            for s in range(8):
                near[leaf, s] = near[leaf, s].T

        loop(2 * q, 2, body)

    def turn_coup(q):
        if q == 0:
            c_coup.wait()

        def body(leaf):
            for s in range(16):
                m = coup[leaf, s].T
                coup_t[leaf, s * 128:s * 128 + 64] = m
                coup_t[leaf, s * 128 + 64:s * 128 + 128] = m

        loop(4 * q, 4, body)

    def turn_onehot():
        def body(leaf):
            span = pl.ds(pl.multiple_of(leaf * 256, 256), 256)
            onehot[span] = onehot[span].T

        loop(0, 16, body)

    def near_some(q):
        def body(k):
            for u in range(4):
                leaf = 4 * k + u
                x = jnp.concatenate([x_buf[near_idx[s, leaf] % 256] for s in range(8)], axis=1)
                near_acc[leaf] = dot(x, near[leaf].reshape(2048, 256), NN)

        loop(q, 1, body)

    def far_all():
        def body(k):
            for u in range(4):
                leaf = 4 * k + u
                c = jnp.concatenate([coef_buf[far_idx[leaf, s] % 256] for s in range(16)], axis=1)
                leaf_acc[leaf] = dot(c, coup_t[leaf], NN)

        loop(0, 4, body)

    def last():
        for leaf in range(16):
            span = slice(leaf * 256, leaf * 256 + 256)
            tree = near_acc[leaf] + dot2(leaf_acc[leaf], basis[leaf], NN)
            high = order[:, span] % 4096 // 256
            spread[:, span] = jnp.concatenate(
                [jnp.where(high == h, tree, 0.0).astype(BF16) for h in range(16)], axis=0
            )
        total = dot(spread[...], onehot[...], NN)
        for h in range(16):
            out_ref[:, h * 256:(h + 1) * 256] = total[h * 16:(h + 1) * 16].astype(BF16)

    node_steps = (node0, node1, node2, node3, node4)
    for token in PLAN:
        kind, number = token[0], int(token[1:] or 0)
        if kind == "x":
            step(0, number)
        elif kind == "c":
            step(1, number)
        elif kind == "n":
            node_steps[number]()
        elif kind == "t":
            turn_near(number)
        elif kind == "d":
            turn_coup(number)
        elif kind == "o":
            turn_onehot()
        elif kind == "N":
            near_some(number)
        elif kind == "F":
            far_all()
        elif kind == "L":
            last()
    for copy in sent:
        copy.wait_send()


def on_device(
    vectors, tree_order, near_blocks, near_index, leaf_basis, leaf_coupling, leaf_far,
    leaf_transfer, node_coupling, node_far, node_transfer, slab_coupling, slab_far_partners,
):
    hbm = pl.BlockSpec(memory_space=pltpu.HBM)
    smem = pl.BlockSpec(memory_space=pltpu.SMEM)
    return pl.pallas_call(
        kernel,
        out_shape=jax.ShapeDtypeStruct((16, 4096), BF16),
        in_specs=[hbm] * 9 + [smem] * 4,
        out_specs=pl.BlockSpec(memory_space=pltpu.VMEM),
        scratch_shapes=[
            pltpu.VMEM((16, 4096), BF16),
            pltpu.VMEM((1, 4096), jnp.int32),
            pltpu.VMEM((16, 8, 256, 256), BF16),
            pltpu.VMEM((16, 64, 256), BF16),
            pltpu.VMEM((16, 16, 64, 64), BF16),
            pltpu.VMEM((16, 64, 64), BF16),
            pltpu.VMEM((1, 8, 64, 64), BF16),
            pltpu.VMEM((1, 64, 64), BF16),
            pltpu.VMEM((1, 2, 64, 64), BF16),
            pltpu.VMEM((4096, 256), BF16),
            pltpu.VMEM((16, 2048, 64), BF16),
            pltpu.VMEM((256, 16, 256), BF16),
            pltpu.VMEM((256, 16, 128), BF16),
            pltpu.VMEM((4, 4, 16, 128), F32),
            pltpu.VMEM((8, 9, 16, 128), F32),
            pltpu.VMEM((16, 16, 256), F32),
            pltpu.VMEM((16, 16, 64), F32),
            pltpu.VMEM((256, 4096), BF16),
            pltpu.SemaphoreType.DMA((8,)),
            pltpu.SemaphoreType.DMA((8,)),
            pltpu.SemaphoreType.DMA((80,)),
            pltpu.SemaphoreType.DMA((80,)),
            pltpu.SemaphoreType.DMA((13,)),
            pltpu.SemaphoreType.DMA((13,)),
        ],
        compiler_params=pltpu.CompilerParams(
            collective_id=0, has_side_effects=True, vmem_limit_bytes=56 << 20
        ),
    )(
        vectors, tree_order.reshape(1, 4096), near_blocks, leaf_basis, leaf_coupling, leaf_transfer,
        node_coupling, node_transfer, slab_coupling,
        near_index.T, leaf_far, node_far, slab_far_partners,
    )


def solution(mesh):
    whole = ("rows", "cols")
    return jax.shard_map(
        on_device,
        mesh=mesh,
        in_specs=(
            P(None, whole), P(whole), P(whole), P(whole), P(whole), P(whole), P(whole),
            P(whole), P(whole), P(whole), P(whole), P("rows"), P("rows"),
        ),
        out_specs=P(None, whole),
        check_vma=False,
    )
```

```python
import jax
import jax.numpy as jnp
from jax import lax
from jax.experimental import pallas as pl
from jax.experimental.pallas import tpu as pltpu
from jax.sharding import PartitionSpec as P

MESH = pl.DeviceIdType.MESH
F32 = jnp.float32
BF16 = jnp.bfloat16

NT = (((1,), (1,)), ((), ()))
NN = (((1,), (0,)), ((), ()))

PLAN = (
    "n0", "c8", "x8", "c9", "x9", "n1", "t0", "c1", "x1", "n2", "t1", "c2", "x2", "t2", "d0",
    "c3", "x3", "t3", "d1", "c4", "x4", "t4", "d2", "c5", "x5", "t5", "d3", "c6", "x6", "n3",
    "t6", "t7", "o", "c7", "F", "n4", "P", "x7", "N0", "N1", "N2", "N3", "L",
)


def dot(a, b, dims):
    return lax.dot_general(a, b, dims, preferred_element_type=F32)


def split2(v):
    high = v.astype(BF16)
    low = (v - high.astype(F32)).astype(BF16)
    return high, low


def dot2(v, b, dims):
    high, low = split2(v)
    rows = v.shape[0]
    both = dot(jnp.concatenate([high, low], axis=0), b, dims)
    return both[:rows] + both[rows:]


def shifted(col, dim, by):
    x, y = col % 4, col // 4
    if dim == 0:
        return y * 4 + (x + by) % 4
    return ((y + by) % 4) * 4 + x


def kernel(
    vec_hbm, ord_hbm, near_hbm, basis_hbm, coup_hbm, ltran_hbm, ncoup_hbm, ntran_hbm, scoup_hbm,
    near_idx_hbm, far_idx_hbm, node_idx_hbm, slab_idx_hbm,
    out_ref,
    near_idx, far_idx, node_idx, slab_idx,
    vec, order, near, basis, coup, ltran, ncoup, ntran, scoup,
    onehot, coup_t, x_buf, coef_buf, node_buf, row_buf, near_acc, leaf_acc, spread,
    in_sem, near_sem, send_sem, recv_sem, nsend, nrecv,
):
    col = lax.axis_index("cols")
    row = lax.axis_index("rows")
    my_x, my_y = col % 4, col // 4

    barrier = pltpu.get_barrier_semaphore()
    partners = [{"cols": shifted(col, dim, by)} for dim in (0, 1) for by in (1, 2, 3)]
    other_core = row + 1 - 2 * (row % 2)
    partners += [{"rows": (row + 2 * by) % 8} for by in (1, 2, 3)] + [{"rows": other_core}]
    for p in partners:
        pl.semaphore_signal(barrier, inc=1, device_id=p, device_id_type=MESH)

    def fetch(src, dst, sem):
        copy = pltpu.make_async_copy(src, dst, sem)
        copy.start()
        return copy

    c_vec = fetch(vec_hbm, vec, in_sem.at[0])
    c_ord = fetch(ord_hbm, order, in_sem.at[1])
    c_lists = [
        fetch(near_idx_hbm, near_idx, in_sem.at[8]),
        fetch(far_idx_hbm, far_idx, in_sem.at[9]),
        fetch(node_idx_hbm, node_idx, in_sem.at[10]),
        fetch(slab_idx_hbm, slab_idx, in_sem.at[11]),
    ]
    c_basis = fetch(basis_hbm, basis, in_sem.at[2])
    c_ltran = fetch(ltran_hbm, ltran, in_sem.at[3])
    c_ntran = fetch(ntran_hbm, ntran, in_sem.at[4])
    c_near = [
        fetch(near_hbm.at[pl.ds(2 * q, 2)], near.at[pl.ds(2 * q, 2)], near_sem.at[q])
        for q in range(8)
    ]
    c_coup = fetch(coup_hbm, coup, in_sem.at[7])
    c_ncoup = fetch(ncoup_hbm, ncoup, in_sem.at[5])
    c_scoup = fetch(scoup_hbm, scoup, in_sem.at[6])

    sent = []
    buffers = (x_buf, coef_buf)

    def chunk_copy(stage, chunk, first, count, to, k):
        span = buffers[stage].at[pl.ds(chunk * 16 + first, count)]
        return pltpu.make_async_remote_copy(
            span, span, send_sem.at[stage * 40 + k], recv_sem.at[stage * 40 + k],
            device_id={"cols": to}, device_id_type=MESH,
        )

    def send(stage, chunk, first, count, to, k):
        copy = chunk_copy(stage, chunk, first, count, to, k)
        copy.start()
        sent.append(copy)

    def arrived(stage, chunk, first, count, k):
        chunk_copy(stage, chunk, first, count, shifted(col, 0, 1), k).wait_recv()

    def at(half, a, b):
        return shifted(shifted(col, half, a), 1 - half, b)

    def key(half, phase, a, t):
        return half * 20 + (0 if phase == 0 else 4 + 4 * a) + t

    def dim_of(half, phase):
        return half if phase == 0 else 1 - half

    def put(stage, half, phase, a):
        d = dim_of(half, phase)
        chunk = at(half, a, 0) if phase else col
        send(stage, chunk, half * 8, 8, shifted(col, d, 1), key(half, phase, a, 0))
        send(stage, chunk, half * 8, 8, shifted(col, d, 3), key(half, phase, a, 1))

    def source(half, phase, a, by):
        return at(half, a, by) if phase else at(half, by, 0)

    def forward(stage, half, phase, a):
        d = dim_of(half, phase)
        chunk = source(half, phase, a, 3)
        arrived(stage, chunk, half * 8, 8, key(half, phase, a, 0))
        send(stage, chunk, half * 8, 4, shifted(col, d, 1), key(half, phase, a, 2))
        chunk = source(half, phase, a, 1)
        arrived(stage, chunk, half * 8, 8, key(half, phase, a, 1))
        send(stage, chunk, half * 8 + 4, 4, shifted(col, d, 3), key(half, phase, a, 3))

    def finish(stage, half, phase, a):
        chunk = source(half, phase, a, 2)
        arrived(stage, chunk, half * 8, 4, key(half, phase, a, 2))
        arrived(stage, chunk, half * 8 + 4, 4, key(half, phase, a, 3))

    def step(stage, number):
        for half in (0, 1):
            if number == 1:
                forward(stage, half, 0, 0)
            if number == 2:
                finish(stage, half, 0, 0)
            if number in (3, 4, 5, 6):
                forward(stage, half, 1, (0, 1, 3, 2)[number - 3])
        for half in (0, 1):
            if number in (0, 8):
                put(stage, half, 0, 0)
            if number == 1:
                put(stage, half, 1, 1)
            if number == 2:
                put(stage, half, 1, 2)
        for half in (0, 1):
            if number in (0, 9):
                put(stage, half, 1, 0)
            if number == 1:
                put(stage, half, 1, 3)
        if number == 7:
            for a in (0, 1, 3, 2):
                for half in (0, 1):
                    finish(stage, half, 1, a)

    c_vec.wait()
    c_ord.wait()
    lhs = jnp.concatenate([vec[:, h * 256:(h + 1) * 256] for h in range(16)], axis=0)
    level = lax.broadcasted_iota(jnp.int32, (256, 256), 0)
    own = col * 16

    def permute(leaf):
        local = order[:, leaf * 256:(leaf + 1) * 256] % 4096
        low = jnp.broadcast_to(local % 256, (256, 256))
        hot = jnp.where(low == level, 1.0, 0.0).astype(BF16)
        onehot[pl.ds(leaf * 256, 256)] = hot
        part = dot(lhs, hot, NN)
        high = local // 256
        x = jnp.zeros((16, 256), F32)
        for h in range(16):
            x = x + jnp.where(high == h, part[h * 16:(h + 1) * 16], 0.0)
        x_buf[own + leaf] = x.astype(BF16)

    for leaf in range(16):
        permute(leaf)

    c_basis.wait()
    for copy in c_lists:
        copy.wait()
    c_ltran.wait()
    c_ntran.wait()
    coefs = []
    for leaf in range(16):
        coef = dot(x_buf[own + leaf], basis[leaf], NT)
        high, low = split2(coef)
        coef_buf[own + leaf] = jnp.concatenate([high, low], axis=1)
        coefs.append(coef)
    node_coef = jnp.zeros((16, 64), F32)
    for leaf in range(16):
        node_coef = node_coef + dot2(coefs[leaf], ltran[leaf], NT)
    node_term = dot2(node_coef, ntran[0], NT)
    pl.semaphore_wait(barrier, len(partners))

    def node_copy(src, k, to):
        return pltpu.make_async_remote_copy(
            src, src, nsend.at[k], nrecv.at[k], device_id=to, device_id_type=MESH
        )

    def node_send(src, k, to):
        copy = node_copy(src, k, to)
        copy.start()
        sent.append(copy)

    def node0():
        node_buf[my_y, my_x] = jnp.concatenate([node_coef, node_term], axis=1)
        for by in (1, 3, 2):
            node_send(node_buf.at[my_y, my_x], by - 1, {"cols": shifted(col, 0, by)})

    def node1():
        for by in (1, 3, 2):
            node_copy(node_buf.at[my_y, (my_x + 4 - by) % 4], by - 1, partners[0]).wait_recv()
        for by in (1, 3, 2):
            node_send(node_buf.at[my_y], 2 + by, {"cols": shifted(col, 1, by)})

    def node2():
        for by in (1, 3, 2):
            node_copy(node_buf.at[(my_y + 4 - by) % 4], 2 + by, partners[0]).wait_recv()
        slab_coef = jnp.zeros((16, 64), F32)
        for m in range(8):
            left, right = node_buf[m // 2, m % 2 * 2], node_buf[m // 2, m % 2 * 2 + 1]
            row_buf[row, m] = jnp.concatenate([left[:, :64], right[:, :64]], axis=1)
            slab_coef = slab_coef + (left[:, 64:] + right[:, 64:])
        row_buf[row, 8] = jnp.concatenate([slab_coef, slab_coef], axis=1)
        for n, by in enumerate((1, 3, 2)):
            node_send(row_buf.at[row], 6 + n, {"rows": (row + 2 * by) % 8})
        node_send(row_buf.at[row], 9, {"rows": other_core})

    def node3():
        for n, by in enumerate((1, 3, 2)):
            source_row = (row + 8 - 2 * by) % 8
            node_copy(row_buf.at[source_row], 6 + n, partners[0]).wait_recv()
            node_send(row_buf.at[source_row], 10 + n, {"rows": other_core})

    def node4():
        node_copy(row_buf.at[other_core], 9, partners[0]).wait_recv()
        for n, by in enumerate((1, 3, 2)):
            source_row = (other_core + 8 - 2 * by) % 8
            node_copy(row_buf.at[source_row], 10 + n, partners[0]).wait_recv()
        c_ncoup.wait()
        c_scoup.wait()
        slab_out = jnp.zeros((16, 64), F32)
        for s in range(2):
            slab_out = slab_out + dot2(row_buf[slab_idx[0, s], 8][:, :64], scoup[0, s], NT)
        node_out = dot2(slab_out, ntran[0], NN)
        lane = lax.broadcasted_iota(jnp.int32, (16, 128), 1)
        for s in range(8):
            d = node_idx[0, s]
            both = row_buf[d // 16, d % 16 // 2]
            both = jnp.where(lane // 64 == d % 2, both, 0.0)
            pair = jnp.concatenate([ncoup[0, s], ncoup[0, s]], axis=1)
            node_out = node_out + dot2(both, pair, NT)
        for leaf in range(16):
            leaf_acc[leaf] = leaf_acc[leaf] + dot2(node_out, ltran[leaf], NN)

    def loop(first, count, body):
        def wrapped(k, carry):
            body(k)
            return carry

        lax.fori_loop(first, first + count, wrapped, 0)

    def turn_near(q):
        c_near[q].wait()

        def body(leaf):
            for s in range(8):
                near[leaf, s] = near[leaf, s].T

        loop(2 * q, 2, body)

    def turn_coup(q):
        if q == 0:
            c_coup.wait()

        def body(leaf):
            for s in range(16):
                m = coup[leaf, s].T
                coup_t[leaf, s * 128:s * 128 + 64] = m
                coup_t[leaf, s * 128 + 64:s * 128 + 128] = m

        loop(4 * q, 4, body)

    def turn_onehot():
        def body(leaf):
            span = pl.ds(pl.multiple_of(leaf * 256, 256), 256)
            onehot[span] = onehot[span].T

        loop(0, 16, body)

    def near_some(q):
        def body(k):
            for u in range(4):
                leaf = 4 * k + u
                x = jnp.concatenate([x_buf[near_idx[s, leaf] % 256] for s in range(8)], axis=1)
                near_acc[leaf] = near_acc[leaf] + dot(x, near[leaf].reshape(2048, 256), NN)

        loop(q, 1, body)

    def far_all():
        def body(k):
            for u in range(4):
                leaf = 4 * k + u
                c = jnp.concatenate([coef_buf[far_idx[leaf, s] % 256] for s in range(16)], axis=1)
                leaf_acc[leaf] = dot(c, coup_t[leaf], NN)

        loop(0, 4, body)

    def far_points():
        for leaf in range(16):
            near_acc[leaf] = dot2(leaf_acc[leaf], basis[leaf], NN)

    def last():
        for leaf in range(16):
            span = slice(leaf * 256, leaf * 256 + 256)
            tree = near_acc[leaf]
            high = order[:, span] % 4096 // 256
            spread[:, span] = jnp.concatenate(
                [jnp.where(high == h, tree, 0.0).astype(BF16) for h in range(16)], axis=0
            )
        total = dot(spread[...], onehot[...], NN)
        for h in range(16):
            out_ref[:, h * 256:(h + 1) * 256] = total[h * 16:(h + 1) * 16].astype(BF16)

    node_steps = (node0, node1, node2, node3, node4)
    for token in PLAN:
        kind, number = token[0], int(token[1:] or 0)
        if kind == "x":
            step(0, number)
        elif kind == "c":
            step(1, number)
        elif kind == "n":
            node_steps[number]()
        elif kind == "t":
            turn_near(number)
        elif kind == "d":
            turn_coup(number)
        elif kind == "o":
            turn_onehot()
        elif kind == "N":
            near_some(number)
        elif kind == "F":
            far_all()
        elif kind == "P":
            far_points()
        elif kind == "L":
            last()
    for copy in sent:
        copy.wait_send()


def on_device(
    vectors, tree_order, near_blocks, near_index, leaf_basis, leaf_coupling, leaf_far,
    leaf_transfer, node_coupling, node_far, node_transfer, slab_coupling, slab_far_partners,
):
    hbm = pl.BlockSpec(memory_space=pltpu.HBM)
    return pl.pallas_call(
        kernel,
        out_shape=pltpu.VMEM((16, 4096), BF16),
        in_specs=[hbm] * 13,
        out_specs=pl.BlockSpec(memory_space=pltpu.VMEM),
        scratch_shapes=[
            pltpu.SMEM((8, 16), jnp.int32),
            pltpu.SMEM((16, 16), jnp.int32),
            pltpu.SMEM((1, 8), jnp.int32),
            pltpu.SMEM((1, 2), jnp.int32),
            pltpu.VMEM((16, 4096), BF16),
            pltpu.VMEM((1, 4096), jnp.int32),
            pltpu.VMEM((16, 8, 256, 256), BF16),
            pltpu.VMEM((16, 64, 256), BF16),
            pltpu.VMEM((16, 16, 64, 64), BF16),
            pltpu.VMEM((16, 64, 64), BF16),
            pltpu.VMEM((1, 8, 64, 64), BF16),
            pltpu.VMEM((1, 64, 64), BF16),
            pltpu.VMEM((1, 2, 64, 64), BF16),
            pltpu.VMEM((4096, 256), BF16),
            pltpu.VMEM((16, 2048, 64), BF16),
            pltpu.VMEM((256, 16, 256), BF16),
            pltpu.VMEM((256, 16, 128), BF16),
            pltpu.VMEM((4, 4, 16, 128), F32),
            pltpu.VMEM((8, 9, 16, 128), F32),
            pltpu.VMEM((16, 16, 256), F32),
            pltpu.VMEM((16, 16, 64), F32),
            pltpu.VMEM((256, 4096), BF16),
            pltpu.SemaphoreType.DMA((12,)),
            pltpu.SemaphoreType.DMA((8,)),
            pltpu.SemaphoreType.DMA((80,)),
            pltpu.SemaphoreType.DMA((80,)),
            pltpu.SemaphoreType.DMA((13,)),
            pltpu.SemaphoreType.DMA((13,)),
        ],
        compiler_params=pltpu.CompilerParams(
            collective_id=0, has_side_effects=True, vmem_limit_bytes=56 << 20
        ),
    )(
        vectors, tree_order.reshape(1, 4096), near_blocks, leaf_basis, leaf_coupling, leaf_transfer,
        node_coupling, node_transfer, slab_coupling,
        near_index.T, leaf_far, node_far, slab_far_partners,
    )


def solution(mesh):
    whole = ("rows", "cols")
    return jax.shard_map(
        on_device,
        mesh=mesh,
        in_specs=(
            P(None, whole), P(whole), P(whole), P(whole), P(whole), P(whole), P(whole),
            P(whole), P(whole), P(whole), P(whole), P("rows"), P("rows"),
        ),
        out_specs=P(None, whole),
        check_vma=False,
    )
```

```python
import jax
import jax.numpy as jnp
from jax import lax
from jax.experimental import pallas as pl
from jax.experimental.pallas import tpu as pltpu
from jax.sharding import PartitionSpec as P

MESH = pl.DeviceIdType.MESH
F32 = jnp.float32
BF16 = jnp.bfloat16

NT = (((1,), (1,)), ((), ()))
NN = (((1,), (0,)), ((), ()))

PLAN = (
    "n0", "c8", "x8", "c9", "x9", "n1", "t0", "c1", "t1", "x1", "t2", "n2", "t3", "c2", "t4",
    "x2", "d0", "c3", "d1", "t5", "x3", "t6", "d2", "c4", "t7", "d3", "x4", "t8", "d4", "c5",
    "t9", "d5", "x5", "t10", "d6", "c6", "t11", "d7", "x6", "n3", "t12", "t13", "t14", "t15",
    "o", "c7", "F", "n4", "P", "x7", "N0", "N1", "N2", "N3", "L",
)


def dot(a, b, dims):
    return lax.dot_general(a, b, dims, preferred_element_type=F32)


def split2(v):
    high = v.astype(BF16)
    low = (v - high.astype(F32)).astype(BF16)
    return high, low


def dot2(v, b, dims):
    high, low = split2(v)
    rows = v.shape[0]
    both = dot(jnp.concatenate([high, low], axis=0), b, dims)
    return both[:rows] + both[rows:]


def shifted(col, dim, by):
    x, y = col % 4, col // 4
    if dim == 0:
        return y * 4 + (x + by) % 4
    return ((y + by) % 4) * 4 + x


def kernel(
    vec_hbm, ord_hbm, near_hbm, basis_hbm, coup_hbm, ltran_hbm, ncoup_hbm, ntran_hbm, scoup_hbm,
    near_idx_hbm, far_idx_hbm, node_idx_hbm, slab_idx_hbm,
    out_ref,
    near_idx, far_idx, node_idx, slab_idx,
    vec, order, near, basis, coup, ltran, ncoup, ntran, scoup,
    onehot, coup_t, x_buf, coef_buf, node_buf, row_buf, near_acc, leaf_acc, spread,
    in_sem, near_sem, send_sem, recv_sem, nsend, nrecv,
):
    col = lax.axis_index("cols")
    row = lax.axis_index("rows")
    my_x, my_y = col % 4, col // 4

    barrier = pltpu.get_barrier_semaphore()
    partners = [{"cols": shifted(col, dim, by)} for dim in (0, 1) for by in (1, 2, 3)]
    other_core = row + 1 - 2 * (row % 2)
    partners += [{"rows": (row + 2 * by) % 8} for by in (1, 2, 3)] + [{"rows": other_core}]
    for p in partners:
        pl.semaphore_signal(barrier, inc=1, device_id=p, device_id_type=MESH)

    def fetch(src, dst, sem):
        copy = pltpu.make_async_copy(src, dst, sem)
        copy.start()
        return copy

    c_vec = fetch(vec_hbm, vec, in_sem.at[0])
    c_ord = fetch(ord_hbm, order, in_sem.at[1])
    c_lists = [
        fetch(near_idx_hbm, near_idx, in_sem.at[8]),
        fetch(far_idx_hbm, far_idx, in_sem.at[9]),
        fetch(node_idx_hbm, node_idx, in_sem.at[10]),
        fetch(slab_idx_hbm, slab_idx, in_sem.at[11]),
    ]
    c_basis = fetch(basis_hbm, basis, in_sem.at[2])
    c_ltran = fetch(ltran_hbm, ltran, in_sem.at[3])
    c_ntran = fetch(ntran_hbm, ntran, in_sem.at[4])
    c_near = [
        fetch(near_hbm.at[pl.ds(2 * q, 2)], near.at[pl.ds(2 * q, 2)], near_sem.at[q])
        for q in range(8)
    ]
    c_coup = fetch(coup_hbm, coup, in_sem.at[7])
    c_ncoup = fetch(ncoup_hbm, ncoup, in_sem.at[5])
    c_scoup = fetch(scoup_hbm, scoup, in_sem.at[6])

    sent = []
    buffers = (x_buf, coef_buf)

    def chunk_copy(stage, chunk, first, count, to, k):
        span = buffers[stage].at[pl.ds(chunk * 16 + first, count)]
        return pltpu.make_async_remote_copy(
            span, span, send_sem.at[stage * 40 + k], recv_sem.at[stage * 40 + k],
            device_id={"cols": to}, device_id_type=MESH,
        )

    def send(stage, chunk, first, count, to, k):
        copy = chunk_copy(stage, chunk, first, count, to, k)
        copy.start()
        sent.append(copy)

    def arrived(stage, chunk, first, count, k):
        chunk_copy(stage, chunk, first, count, shifted(col, 0, 1), k).wait_recv()

    def at(half, a, b):
        return shifted(shifted(col, half, a), 1 - half, b)

    def key(half, phase, a, t):
        return half * 20 + (0 if phase == 0 else 4 + 4 * a) + t

    def dim_of(half, phase):
        return half if phase == 0 else 1 - half

    def put(stage, half, phase, a):
        d = dim_of(half, phase)
        chunk = at(half, a, 0) if phase else col
        send(stage, chunk, half * 8, 8, shifted(col, d, 1), key(half, phase, a, 0))
        send(stage, chunk, half * 8, 8, shifted(col, d, 3), key(half, phase, a, 1))

    def source(half, phase, a, by):
        return at(half, a, by) if phase else at(half, by, 0)

    def forward(stage, half, phase, a):
        d = dim_of(half, phase)
        chunk = source(half, phase, a, 3)
        arrived(stage, chunk, half * 8, 8, key(half, phase, a, 0))
        send(stage, chunk, half * 8, 4, shifted(col, d, 1), key(half, phase, a, 2))
        chunk = source(half, phase, a, 1)
        arrived(stage, chunk, half * 8, 8, key(half, phase, a, 1))
        send(stage, chunk, half * 8 + 4, 4, shifted(col, d, 3), key(half, phase, a, 3))

    def finish(stage, half, phase, a):
        chunk = source(half, phase, a, 2)
        arrived(stage, chunk, half * 8, 4, key(half, phase, a, 2))
        arrived(stage, chunk, half * 8 + 4, 4, key(half, phase, a, 3))

    def step(stage, number):
        for half in (0, 1):
            if number == 1:
                forward(stage, half, 0, 0)
            if number == 2:
                finish(stage, half, 0, 0)
            if number in (3, 4, 5, 6):
                forward(stage, half, 1, (0, 1, 3, 2)[number - 3])
        for half in (0, 1):
            if number in (0, 8):
                put(stage, half, 0, 0)
            if number == 1:
                put(stage, half, 1, 1)
            if number == 2:
                put(stage, half, 1, 2)
        for half in (0, 1):
            if number in (0, 9):
                put(stage, half, 1, 0)
            if number == 1:
                put(stage, half, 1, 3)
        if number == 7:
            for a in (0, 1, 3, 2):
                for half in (0, 1):
                    finish(stage, half, 1, a)

    c_vec.wait()
    c_ord.wait()
    lhs = jnp.concatenate([vec[:, h * 256:(h + 1) * 256] for h in range(16)], axis=0)
    level = lax.broadcasted_iota(jnp.int32, (256, 256), 0)
    own = col * 16

    def permute(leaf):
        local = order[:, leaf * 256:(leaf + 1) * 256] % 4096
        low = jnp.broadcast_to(local % 256, (256, 256))
        hot = jnp.where(low == level, 1.0, 0.0).astype(BF16)
        onehot[pl.ds(leaf * 256, 256)] = hot
        part = dot(lhs, hot, NN)
        high = local // 256
        x = jnp.zeros((16, 256), F32)
        for h in range(16):
            x = x + jnp.where(high == h, part[h * 16:(h + 1) * 16], 0.0)
        x_buf[own + leaf] = x.astype(BF16)

    for leaf in range(16):
        permute(leaf)

    c_basis.wait()
    for copy in c_lists:
        copy.wait()
    c_ltran.wait()
    c_ntran.wait()
    coefs = []
    for leaf in range(16):
        coef = dot(x_buf[own + leaf], basis[leaf], NT)
        high, low = split2(coef)
        coef_buf[own + leaf] = jnp.concatenate([high, low], axis=1)
        coefs.append(coef)
    node_coef = jnp.zeros((16, 64), F32)
    for leaf in range(16):
        node_coef = node_coef + dot2(coefs[leaf], ltran[leaf], NT)
    node_term = dot2(node_coef, ntran[0], NT)
    pl.semaphore_wait(barrier, len(partners))

    def node_copy(src, k, to):
        return pltpu.make_async_remote_copy(
            src, src, nsend.at[k], nrecv.at[k], device_id=to, device_id_type=MESH
        )

    def node_send(src, k, to):
        copy = node_copy(src, k, to)
        copy.start()
        sent.append(copy)

    def node0():
        node_buf[my_y, my_x] = jnp.concatenate([node_coef, node_term], axis=1)
        for by in (1, 3, 2):
            node_send(node_buf.at[my_y, my_x], by - 1, {"cols": shifted(col, 0, by)})

    def node1():
        for by in (1, 3, 2):
            node_copy(node_buf.at[my_y, (my_x + 4 - by) % 4], by - 1, partners[0]).wait_recv()
        for by in (1, 3, 2):
            node_send(node_buf.at[my_y], 2 + by, {"cols": shifted(col, 1, by)})

    def node2():
        for by in (1, 3, 2):
            node_copy(node_buf.at[(my_y + 4 - by) % 4], 2 + by, partners[0]).wait_recv()
        slab_coef = jnp.zeros((16, 64), F32)
        for m in range(8):
            left, right = node_buf[m // 2, m % 2 * 2], node_buf[m // 2, m % 2 * 2 + 1]
            row_buf[row, m] = jnp.concatenate([left[:, :64], right[:, :64]], axis=1)
            slab_coef = slab_coef + (left[:, 64:] + right[:, 64:])
        row_buf[row, 8] = jnp.concatenate([slab_coef, slab_coef], axis=1)
        for n, by in enumerate((1, 3, 2)):
            node_send(row_buf.at[row], 6 + n, {"rows": (row + 2 * by) % 8})
        node_send(row_buf.at[row], 9, {"rows": other_core})

    def node3():
        for n, by in enumerate((1, 3, 2)):
            source_row = (row + 8 - 2 * by) % 8
            node_copy(row_buf.at[source_row], 6 + n, partners[0]).wait_recv()
            node_send(row_buf.at[source_row], 10 + n, {"rows": other_core})

    def node4():
        node_copy(row_buf.at[other_core], 9, partners[0]).wait_recv()
        for n, by in enumerate((1, 3, 2)):
            source_row = (other_core + 8 - 2 * by) % 8
            node_copy(row_buf.at[source_row], 10 + n, partners[0]).wait_recv()
        c_ncoup.wait()
        c_scoup.wait()
        slab_out = jnp.zeros((16, 64), F32)
        for s in range(2):
            slab_out = slab_out + dot2(row_buf[slab_idx[0, s], 8][:, :64], scoup[0, s], NT)
        node_out = dot2(slab_out, ntran[0], NN)
        lane = lax.broadcasted_iota(jnp.int32, (16, 128), 1)
        for s in range(8):
            d = node_idx[0, s]
            both = row_buf[d // 16, d % 16 // 2]
            both = jnp.where(lane // 64 == d % 2, both, 0.0)
            pair = jnp.concatenate([ncoup[0, s], ncoup[0, s]], axis=1)
            node_out = node_out + dot2(both, pair, NT)
        for leaf in range(16):
            leaf_acc[leaf] = leaf_acc[leaf] + dot2(node_out, ltran[leaf], NN)

    def loop(first, count, body):
        def wrapped(k, carry):
            body(k)
            return carry

        lax.fori_loop(first, first + count, wrapped, 0)

    def turn_near(q):
        if q % 2 == 0:
            c_near[q // 2].wait()
        for s in range(8):
            near[q, s] = near[q, s].T

    def turn_coup(q):
        if q == 0:
            c_coup.wait()

        def body(leaf):
            for s in range(16):
                m = coup[leaf, s].T
                coup_t[leaf, s * 128:s * 128 + 64] = m
                coup_t[leaf, s * 128 + 64:s * 128 + 128] = m

        loop(2 * q, 2, body)

    def turn_onehot():
        def body(leaf):
            span = pl.ds(pl.multiple_of(leaf * 256, 256), 256)
            onehot[span] = onehot[span].T

        loop(0, 16, body)

    def near_some(q):
        def body(k):
            for u in range(4):
                leaf = 4 * k + u
                x = jnp.concatenate([x_buf[near_idx[s, leaf] % 256] for s in range(8)], axis=1)
                near_acc[leaf] = near_acc[leaf] + dot(x, near[leaf].reshape(2048, 256), NN)

        loop(q, 1, body)

    def far_all():
        def body(k):
            for u in range(4):
                leaf = 4 * k + u
                c = jnp.concatenate([coef_buf[far_idx[leaf, s] % 256] for s in range(16)], axis=1)
                leaf_acc[leaf] = dot(c, coup_t[leaf], NN)

        loop(0, 4, body)

    def far_points():
        for leaf in range(16):
            near_acc[leaf] = dot2(leaf_acc[leaf], basis[leaf], NN)

    def last():
        for leaf in range(16):
            span = slice(leaf * 256, leaf * 256 + 256)
            tree = near_acc[leaf]
            high = order[:, span] % 4096 // 256
            spread[:, span] = jnp.concatenate(
                [jnp.where(high == h, tree, 0.0).astype(BF16) for h in range(16)], axis=0
            )
        total = dot(spread[...], onehot[...], NN)
        for h in range(16):
            out_ref[:, h * 256:(h + 1) * 256] = total[h * 16:(h + 1) * 16].astype(BF16)

    node_steps = (node0, node1, node2, node3, node4)
    for token in PLAN:
        kind, number = token[0], int(token[1:] or 0)
        if kind == "x":
            step(0, number)
        elif kind == "c":
            step(1, number)
        elif kind == "n":
            node_steps[number]()
        elif kind == "t":
            turn_near(number)
        elif kind == "d":
            turn_coup(number)
        elif kind == "o":
            turn_onehot()
        elif kind == "N":
            near_some(number)
        elif kind == "F":
            far_all()
        elif kind == "P":
            far_points()
        elif kind == "L":
            last()
    for copy in sent:
        copy.wait_send()


def on_device(
    vectors, tree_order, near_blocks, near_index, leaf_basis, leaf_coupling, leaf_far,
    leaf_transfer, node_coupling, node_far, node_transfer, slab_coupling, slab_far_partners,
):
    hbm = pl.BlockSpec(memory_space=pltpu.HBM)
    return pl.pallas_call(
        kernel,
        out_shape=pltpu.VMEM((16, 4096), BF16),
        in_specs=[hbm] * 13,
        out_specs=pl.BlockSpec(memory_space=pltpu.VMEM),
        scratch_shapes=[
            pltpu.SMEM((8, 16), jnp.int32),
            pltpu.SMEM((16, 16), jnp.int32),
            pltpu.SMEM((1, 8), jnp.int32),
            pltpu.SMEM((1, 2), jnp.int32),
            pltpu.VMEM((16, 4096), BF16),
            pltpu.VMEM((1, 4096), jnp.int32),
            pltpu.VMEM((16, 8, 256, 256), BF16),
            pltpu.VMEM((16, 64, 256), BF16),
            pltpu.VMEM((16, 16, 64, 64), BF16),
            pltpu.VMEM((16, 64, 64), BF16),
            pltpu.VMEM((1, 8, 64, 64), BF16),
            pltpu.VMEM((1, 64, 64), BF16),
            pltpu.VMEM((1, 2, 64, 64), BF16),
            pltpu.VMEM((4096, 256), BF16),
            pltpu.VMEM((16, 2048, 64), BF16),
            pltpu.VMEM((256, 16, 256), BF16),
            pltpu.VMEM((256, 16, 128), BF16),
            pltpu.VMEM((4, 4, 16, 128), F32),
            pltpu.VMEM((8, 9, 16, 128), F32),
            pltpu.VMEM((16, 16, 256), F32),
            pltpu.VMEM((16, 16, 64), F32),
            pltpu.VMEM((256, 4096), BF16),
            pltpu.SemaphoreType.DMA((12,)),
            pltpu.SemaphoreType.DMA((8,)),
            pltpu.SemaphoreType.DMA((80,)),
            pltpu.SemaphoreType.DMA((80,)),
            pltpu.SemaphoreType.DMA((13,)),
            pltpu.SemaphoreType.DMA((13,)),
        ],
        compiler_params=pltpu.CompilerParams(
            collective_id=0, has_side_effects=True, vmem_limit_bytes=56 << 20
        ),
    )(
        vectors, tree_order.reshape(1, 4096), near_blocks, leaf_basis, leaf_coupling, leaf_transfer,
        node_coupling, node_transfer, slab_coupling,
        near_index.T, leaf_far, node_far, slab_far_partners,
    )


def solution(mesh):
    whole = ("rows", "cols")
    return jax.shard_map(
        on_device,
        mesh=mesh,
        in_specs=(
            P(None, whole), P(whole), P(whole), P(whole), P(whole), P(whole), P(whole),
            P(whole), P(whole), P(whole), P(whole), P("rows"), P("rows"),
        ),
        out_specs=P(None, whole),
        check_vma=False,
    )
```

```python
import jax
import jax.numpy as jnp
from jax import lax
from jax.experimental import pallas as pl
from jax.experimental.pallas import tpu as pltpu
from jax.sharding import PartitionSpec as P

MESH = pl.DeviceIdType.MESH
F32 = jnp.float32
BF16 = jnp.bfloat16

NT = (((1,), (1,)), ((), ()))
NN = (((1,), (0,)), ((), ()))

PLAN = (
    "n0", "c8", "x8", "c9", "x9", "n1", "t0", "c1", "t1", "x1", "t2", "n2", "t3", "c2", "t4",
    "x2", "d0", "c3", "d1", "t5", "x3", "t6", "d2", "c4", "t7", "d3", "x4", "t8", "d4", "c5",
    "t9", "d5", "x5", "t10", "d6", "c6", "t11", "d7", "x6", "n3", "t12", "t13", "t14", "t15",
    "o", "c7", "F", "n4", "P", "x7", "N0", "N1", "N2", "N3", "L",
)


def dot(a, b, dims):
    return lax.dot_general(a, b, dims, preferred_element_type=F32)


def split2(v):
    high = v.astype(BF16)
    low = (v - high.astype(F32)).astype(BF16)
    return high, low


def dot2(v, b, dims):
    high, low = split2(v)
    rows = v.shape[0]
    both = dot(jnp.concatenate([high, low], axis=0), b, dims)
    return both[:rows] + both[rows:]


def shifted(col, dim, by):
    x, y = col % 4, col // 4
    if dim == 0:
        return y * 4 + (x + by) % 4
    return ((y + by) % 4) * 4 + x


def kernel(
    vec_hbm, ord_hbm, near_hbm, basis_hbm, coup_hbm, ltran_hbm, ncoup_hbm, ntran_hbm, scoup_hbm,
    near_idx_hbm, far_idx_hbm, node_idx_hbm, slab_idx_hbm,
    out_ref,
    near_idx, far_idx, node_idx, slab_idx,
    vec, order, near, basis, coup, ltran, ncoup, ntran, scoup,
    onehot, coup_t, x_buf, coef_buf, node_buf, row_buf, near_acc, leaf_acc, spread,
    in_sem, near_sem, send_sem, recv_sem, nsend, nrecv,
):
    col = lax.axis_index("cols")
    row = lax.axis_index("rows")
    my_x, my_y = col % 4, col // 4

    barrier = pltpu.get_barrier_semaphore()
    partners = [{"cols": shifted(col, dim, by)} for dim in (0, 1) for by in (1, 2, 3)]
    other_core = row + 1 - 2 * (row % 2)
    partners += [{"rows": (row + 2 * by) % 8} for by in (1, 2, 3)] + [{"rows": other_core}]
    for p in partners[6:] + partners[:6]:
        pl.semaphore_signal(barrier, inc=1, device_id=p, device_id_type=MESH)

    def fetch(src, dst, sem):
        copy = pltpu.make_async_copy(src, dst, sem)
        copy.start()
        return copy

    c_vec = fetch(vec_hbm, vec, in_sem.at[0])
    c_ord = fetch(ord_hbm, order, in_sem.at[1])
    c_lists = [
        fetch(near_idx_hbm, near_idx, in_sem.at[8]),
        fetch(far_idx_hbm, far_idx, in_sem.at[9]),
        fetch(node_idx_hbm, node_idx, in_sem.at[10]),
        fetch(slab_idx_hbm, slab_idx, in_sem.at[11]),
    ]
    c_basis = fetch(basis_hbm, basis, in_sem.at[2])
    c_ltran = fetch(ltran_hbm, ltran, in_sem.at[3])
    c_ntran = fetch(ntran_hbm, ntran, in_sem.at[4])
    c_near = [
        fetch(near_hbm.at[pl.ds(2 * q, 2)], near.at[pl.ds(2 * q, 2)], near_sem.at[q])
        for q in range(8)
    ]
    c_coup = fetch(coup_hbm, coup, in_sem.at[7])
    c_ncoup = fetch(ncoup_hbm, ncoup, in_sem.at[5])
    c_scoup = fetch(scoup_hbm, scoup, in_sem.at[6])

    sent = []
    buffers = (x_buf, coef_buf)

    def chunk_copy(stage, chunk, first, count, to, k):
        span = buffers[stage].at[pl.ds(chunk * 16 + first, count)]
        return pltpu.make_async_remote_copy(
            span, span, send_sem.at[stage * 40 + k], recv_sem.at[stage * 40 + k],
            device_id={"cols": to}, device_id_type=MESH,
        )

    def send(stage, chunk, first, count, to, k):
        copy = chunk_copy(stage, chunk, first, count, to, k)
        copy.start()
        sent.append(copy)

    def arrived(stage, chunk, first, count, k):
        chunk_copy(stage, chunk, first, count, shifted(col, 0, 1), k).wait_recv()

    def at(half, a, b):
        return shifted(shifted(col, half, a), 1 - half, b)

    def key(half, phase, a, t):
        return half * 20 + (0 if phase == 0 else 4 + 4 * a) + t

    def dim_of(half, phase):
        return half if phase == 0 else 1 - half

    def put(stage, half, phase, a):
        d = dim_of(half, phase)
        chunk = at(half, a, 0) if phase else col
        send(stage, chunk, half * 8, 8, shifted(col, d, 1), key(half, phase, a, 0))
        send(stage, chunk, half * 8, 8, shifted(col, d, 3), key(half, phase, a, 1))

    def source(half, phase, a, by):
        return at(half, a, by) if phase else at(half, by, 0)

    def forward(stage, half, phase, a):
        d = dim_of(half, phase)
        chunk = source(half, phase, a, 3)
        arrived(stage, chunk, half * 8, 8, key(half, phase, a, 0))
        send(stage, chunk, half * 8, 4, shifted(col, d, 1), key(half, phase, a, 2))
        chunk = source(half, phase, a, 1)
        arrived(stage, chunk, half * 8, 8, key(half, phase, a, 1))
        send(stage, chunk, half * 8 + 4, 4, shifted(col, d, 3), key(half, phase, a, 3))

    def finish(stage, half, phase, a):
        chunk = source(half, phase, a, 2)
        arrived(stage, chunk, half * 8, 4, key(half, phase, a, 2))
        arrived(stage, chunk, half * 8 + 4, 4, key(half, phase, a, 3))

    def step(stage, number):
        for half in (0, 1):
            if number == 1:
                forward(stage, half, 0, 0)
            if number == 2:
                finish(stage, half, 0, 0)
            if number in (3, 4, 5, 6):
                forward(stage, half, 1, (0, 1, 3, 2)[number - 3])
        for half in (0, 1):
            if number in (0, 8):
                put(stage, half, 0, 0)
            if number == 1:
                put(stage, half, 1, 1)
            if number == 2:
                put(stage, half, 1, 2)
        for half in (0, 1):
            if number in (0, 9):
                put(stage, half, 1, 0)
            if number == 1:
                put(stage, half, 1, 3)
        if number == 7:
            for a in (0, 1, 3, 2):
                for half in (0, 1):
                    finish(stage, half, 1, a)

    c_vec.wait()
    c_ord.wait()
    lhs = jnp.concatenate([vec[:, h * 256:(h + 1) * 256] for h in range(16)], axis=0)
    level = lax.broadcasted_iota(jnp.int32, (256, 256), 0)
    own = col * 16

    def permute(leaf):
        local = order[:, leaf * 256:(leaf + 1) * 256] % 4096
        low = jnp.broadcast_to(local % 256, (256, 256))
        hot = jnp.where(low == level, 1.0, 0.0).astype(BF16)
        onehot[pl.ds(leaf * 256, 256)] = hot
        part = dot(lhs, hot, NN)
        high = local // 256
        x = jnp.zeros((16, 256), F32)
        for h in range(16):
            x = x + jnp.where(high == h, part[h * 16:(h + 1) * 16], 0.0)
        x_buf[own + leaf] = x.astype(BF16)

    for leaf in range(16):
        permute(leaf)

    c_basis.wait()
    for copy in c_lists:
        copy.wait()
    c_ltran.wait()
    c_ntran.wait()
    coefs = []
    for leaf in range(16):
        coef = dot(x_buf[own + leaf], basis[leaf], NT)
        high, low = split2(coef)
        coef_buf[own + leaf] = jnp.concatenate([high, low], axis=1)
        coefs.append(coef)
    node_coef = jnp.zeros((16, 64), F32)
    for leaf in range(16):
        node_coef = node_coef + dot2(coefs[leaf], ltran[leaf], NT)
    node_term = dot2(node_coef, ntran[0], NT)
    pl.semaphore_wait(barrier, len(partners))

    def node_copy(src, k, to):
        return pltpu.make_async_remote_copy(
            src, src, nsend.at[k], nrecv.at[k], device_id=to, device_id_type=MESH
        )

    def node_send(src, k, to):
        copy = node_copy(src, k, to)
        copy.start()
        sent.append(copy)

    def node0():
        node_buf[my_y, my_x] = jnp.concatenate([node_coef, node_term], axis=1)
        for by in (1, 3, 2):
            node_send(node_buf.at[my_y, my_x], by - 1, {"cols": shifted(col, 0, by)})

    def node1():
        for by in (1, 3, 2):
            node_copy(node_buf.at[my_y, (my_x + 4 - by) % 4], by - 1, partners[0]).wait_recv()
        for by in (1, 3, 2):
            node_send(node_buf.at[my_y], 2 + by, {"cols": shifted(col, 1, by)})

    def node2():
        for by in (1, 3, 2):
            node_copy(node_buf.at[(my_y + 4 - by) % 4], 2 + by, partners[0]).wait_recv()
        slab_coef = jnp.zeros((16, 64), F32)
        for m in range(8):
            left, right = node_buf[m // 2, m % 2 * 2], node_buf[m // 2, m % 2 * 2 + 1]
            row_buf[row, m] = jnp.concatenate([left[:, :64], right[:, :64]], axis=1)
            slab_coef = slab_coef + (left[:, 64:] + right[:, 64:])
        row_buf[row, 8] = jnp.concatenate([slab_coef, slab_coef], axis=1)
        for n, by in enumerate((1, 3, 2)):
            node_send(row_buf.at[row], 6 + n, {"rows": (row + 2 * by) % 8})
        node_send(row_buf.at[row], 9, {"rows": other_core})

    def node3():
        for n, by in enumerate((1, 3, 2)):
            source_row = (row + 8 - 2 * by) % 8
            node_copy(row_buf.at[source_row], 6 + n, partners[0]).wait_recv()
            node_send(row_buf.at[source_row], 10 + n, {"rows": other_core})

    def node4():
        node_copy(row_buf.at[other_core], 9, partners[0]).wait_recv()
        for n, by in enumerate((1, 3, 2)):
            source_row = (other_core + 8 - 2 * by) % 8
            node_copy(row_buf.at[source_row], 10 + n, partners[0]).wait_recv()
        c_ncoup.wait()
        c_scoup.wait()
        slab_out = jnp.zeros((16, 64), F32)
        for s in range(2):
            slab_out = slab_out + dot2(row_buf[slab_idx[0, s], 8][:, :64], scoup[0, s], NT)
        node_out = dot2(slab_out, ntran[0], NN)
        lane = lax.broadcasted_iota(jnp.int32, (16, 128), 1)
        for s in range(8):
            d = node_idx[0, s]
            both = row_buf[d // 16, d % 16 // 2]
            both = jnp.where(lane // 64 == d % 2, both, 0.0)
            pair = jnp.concatenate([ncoup[0, s], ncoup[0, s]], axis=1)
            node_out = node_out + dot2(both, pair, NT)
        for leaf in range(16):
            leaf_acc[leaf] = leaf_acc[leaf] + dot2(node_out, ltran[leaf], NN)

    def loop(first, count, body):
        def wrapped(k, carry):
            body(k)
            return carry

        lax.fori_loop(first, first + count, wrapped, 0)

    def turn_near(q):
        if q % 2 == 0:
            c_near[q // 2].wait()
        for s in range(8):
            near[q, s] = near[q, s].T

    def turn_coup(q):
        if q == 0:
            c_coup.wait()

        def body(leaf):
            for s in range(16):
                m = coup[leaf, s].T
                coup_t[leaf, s * 128:s * 128 + 64] = m
                coup_t[leaf, s * 128 + 64:s * 128 + 128] = m

        loop(2 * q, 2, body)

    def turn_onehot():
        def body(leaf):
            span = pl.ds(pl.multiple_of(leaf * 256, 256), 256)
            onehot[span] = onehot[span].T

        loop(0, 16, body)

    def near_some(q):
        def body(k):
            for u in range(4):
                leaf = 4 * k + u
                x = jnp.concatenate([x_buf[near_idx[s, leaf] % 256] for s in range(8)], axis=1)
                near_acc[leaf] = near_acc[leaf] + dot(x, near[leaf].reshape(2048, 256), NN)

        loop(q, 1, body)

    def far_all():
        def body(k):
            for u in range(4):
                leaf = 4 * k + u
                c = jnp.concatenate([coef_buf[far_idx[leaf, s] % 256] for s in range(16)], axis=1)
                leaf_acc[leaf] = dot(c, coup_t[leaf], NN)

        loop(0, 4, body)

    def far_points():
        for leaf in range(16):
            near_acc[leaf] = dot2(leaf_acc[leaf], basis[leaf], NN)

    def last():
        for leaf in range(16):
            span = slice(leaf * 256, leaf * 256 + 256)
            tree = near_acc[leaf]
            high = order[:, span] % 4096 // 256
            spread[:, span] = jnp.concatenate(
                [jnp.where(high == h, tree, 0.0).astype(BF16) for h in range(16)], axis=0
            )
        total = dot(spread[...], onehot[...], NN)
        for h in range(16):
            out_ref[:, h * 256:(h + 1) * 256] = total[h * 16:(h + 1) * 16].astype(BF16)

    node_steps = (node0, node1, node2, node3, node4)
    for token in PLAN:
        kind, number = token[0], int(token[1:] or 0)
        if kind == "x":
            step(0, number)
        elif kind == "c":
            step(1, number)
        elif kind == "n":
            node_steps[number]()
        elif kind == "t":
            turn_near(number)
        elif kind == "d":
            turn_coup(number)
        elif kind == "o":
            turn_onehot()
        elif kind == "N":
            near_some(number)
        elif kind == "F":
            far_all()
        elif kind == "P":
            far_points()
        elif kind == "L":
            last()
    for copy in sent:
        copy.wait_send()


def on_device(
    vectors, tree_order, near_blocks, near_index, leaf_basis, leaf_coupling, leaf_far,
    leaf_transfer, node_coupling, node_far, node_transfer, slab_coupling, slab_far_partners,
):
    hbm = pl.BlockSpec(memory_space=pltpu.HBM)
    return pl.pallas_call(
        kernel,
        out_shape=pltpu.VMEM((16, 4096), BF16),
        in_specs=[hbm] * 13,
        out_specs=pl.BlockSpec(memory_space=pltpu.VMEM),
        scratch_shapes=[
            pltpu.SMEM((8, 16), jnp.int32),
            pltpu.SMEM((16, 16), jnp.int32),
            pltpu.SMEM((1, 8), jnp.int32),
            pltpu.SMEM((1, 2), jnp.int32),
            pltpu.VMEM((16, 4096), BF16),
            pltpu.VMEM((1, 4096), jnp.int32),
            pltpu.VMEM((16, 8, 256, 256), BF16),
            pltpu.VMEM((16, 64, 256), BF16),
            pltpu.VMEM((16, 16, 64, 64), BF16),
            pltpu.VMEM((16, 64, 64), BF16),
            pltpu.VMEM((1, 8, 64, 64), BF16),
            pltpu.VMEM((1, 64, 64), BF16),
            pltpu.VMEM((1, 2, 64, 64), BF16),
            pltpu.VMEM((4096, 256), BF16),
            pltpu.VMEM((16, 2048, 64), BF16),
            pltpu.VMEM((256, 16, 256), BF16),
            pltpu.VMEM((256, 16, 128), BF16),
            pltpu.VMEM((4, 4, 16, 128), F32),
            pltpu.VMEM((8, 9, 16, 128), F32),
            pltpu.VMEM((16, 16, 256), F32),
            pltpu.VMEM((16, 16, 64), F32),
            pltpu.VMEM((256, 4096), BF16),
            pltpu.SemaphoreType.DMA((12,)),
            pltpu.SemaphoreType.DMA((8,)),
            pltpu.SemaphoreType.DMA((80,)),
            pltpu.SemaphoreType.DMA((80,)),
            pltpu.SemaphoreType.DMA((13,)),
            pltpu.SemaphoreType.DMA((13,)),
        ],
        compiler_params=pltpu.CompilerParams(
            collective_id=0, has_side_effects=True, vmem_limit_bytes=56 << 20
        ),
    )(
        vectors, tree_order.reshape(1, 4096), near_blocks, leaf_basis, leaf_coupling, leaf_transfer,
        node_coupling, node_transfer, slab_coupling,
        near_index.T, leaf_far, node_far, slab_far_partners,
    )


def solution(mesh):
    whole = ("rows", "cols")
    return jax.shard_map(
        on_device,
        mesh=mesh,
        in_specs=(
            P(None, whole), P(whole), P(whole), P(whole), P(whole), P(whole), P(whole),
            P(whole), P(whole), P(whole), P(whole), P("rows"), P("rows"),
        ),
        out_specs=P(None, whole),
        check_vma=False,
    )
```
